32 devices in a mesh: sfc: 8 (over y, x, core), grp: 4 (over z).
Axes of the slice: x: 2, y: 2, z: 4, core: 2. Of those that a mesh axis runs over, the one named last changes fastest.
Arguments:
- bin_points: float32 [32768, 5, 256], P(('sfc', 'grp')), may hold values from -1 to 1, as said below
- bin_plan: int32 [32768, 1], P(('sfc', 'grp')), may hold values from 0 to 7; in each aligned block of 1024 rows (0 to 1023, 1024 to 2047, ...) at most 128 rows name the same one
- bin_leaf: int32 [32768], P(('sfc', 'grp')), may hold values from 0 to 255
- leaf_slots: int32 [8, 8, 128], P('sfc', None, 'grp'), may hold values from 0 to 127, each once within a row
- box_slots: int32 [8, 8, 16], P('sfc'), may hold values from 0 to 15, each once within a row
- parent_cone: int32 [8, 128], P('sfc'), may hold values from 0 to 15
- box_cone: int32 [8, 16], P('sfc'), may hold values from 0 to 15
- cone_angles: float32 [16, 2], replicated, may hold values from -3.140625 to 3.140625
Outputs:
- leaf_expansions: float32 [8192, 2, 512], P(('sfc', 'grp'))
- level_one: float32 [1024, 2, 512], P(('sfc', 'grp'))
- level_two: float32 [128, 2, 512], P(('sfc', 'grp'))
The draws below stay inside these ranges and needn't reach their ends.
Inputs may be any that keep to these rules, and one draw needn't show every extreme that they name: `bin_plan`: among the rows of one device no value is named by more than 128 rows, a bound that some block reaches. Each row leaf_slots[s, o, :] names every level-one box of segment s once, so every level-one box has exactly one child of each octant. Each row box_slots[s, o, :] names every level-two box of segment s once. `bin_points`: coordinates lie within -1 to 1 and densities within -0.4 to 0.4.
All inputs are finite; a program needn't handle non-finite values.
Results may differ from the reference program's by a relative error of at most 0.0039.
Values sent between devices are 32-bit elements; how exact they have to be, the bound alone decides.
A program may use at most 320 MiB of HBM per device.

```python
import math
import jax
import jax.numpy as jnp
import numpy as np
from jax import lax

PTS = 256
CONES = 16
BINS_DEV = 1024
LEAF_DEV = 256
CAP = 128
BINS = 32768
PAR1 = 128
PAR2 = 16
N_SFC = 8
N_GRP = 4


def draw_bin_points(key, part):
    coord_key = jax.random.fold_in(key, 11)
    dens_key = jax.random.fold_in(key, 23)
    coords = jax.random.uniform(coord_key, (BINS, 3, PTS), jnp.float32, -1.0, 1.0)
    density = jnp.clip(0.05 * jax.random.normal(dens_key, (BINS, 2, PTS), jnp.float32), -0.4, 0.4)
    return jnp.concatenate([coords, density], axis=1).astype(jnp.float32)


def set_ends(values, rng, least, top_value):
    dims = values.shape
    spot = [jax.random.randint(jax.random.fold_in(rng, axis), (), 0, dims[axis]) for axis in range(len(dims))]
    values = values.at[tuple(spot)].set(least)
    longest = dims.index(max(dims))
    spot[longest] = (spot[longest] + 1) % dims[longest]
    return values.at[tuple(spot)].set(top_value)


def routed_block(own_key, own, number, rows, amount, top, reach, slope):
    ranking = jax.random.permutation(own_key, amount)
    crowded, ordinary = shares(amount, rows * top, reach, slope, True), shares(amount, rows * top, reach, slope, False)
    places = jnp.arange(amount)

    def named(lengths, offset_by):
        used = int((lengths > 0).sum())
        fixed = max(1, used // 4)
        moved = fixed + (places - fixed + offset_by * (used - fixed)) % max(1, amount - fixed)
        return jnp.zeros((amount,), jnp.int32).at[ranking[jnp.where(places < fixed, places, moved)]].set(jnp.asarray(lengths, jnp.int32))

    lengths = jnp.where(number % 4 == 0, named(crowded, number // 4), named(ordinary, number - number // 4 - 1))
    mixed = jax.random.permutation(jax.random.fold_in(own, 3), amount)
    donor, receiver = mixed[0:amount // 2 * 2:2], mixed[1:amount // 2 * 2:2]
    room = jnp.minimum(lengths[donor] - 1, reach - lengths[receiver]) // 2
    room = jnp.where((donor == ranking[0]) | (receiver == ranking[0]) | (lengths[receiver] == 0), 0, jnp.maximum(room, 0))
    moved = jax.random.randint(jax.random.fold_in(own, 4), (amount // 2,), 0, 1 << 20) % (room + 1)
    lengths = lengths.at[donor].add(-moved).at[receiver].add(moved)
    items = jnp.searchsorted(jnp.cumsum(lengths), jnp.arange(rows * top), side="right").astype(jnp.int32)
    table = items.reshape(top, rows).T
    table = table[jax.random.permutation(jax.random.fold_in(own, 1), rows)]
    offset_by = jax.random.randint(jax.random.fold_in(own, 2), (rows, 1), 0, top)
    return jnp.take_along_axis(table, (jnp.arange(top)[None, :] + offset_by) % top, axis=1)


def shares(amount, total, reach, skew, full):
    portions = [(1 << 20) // math.isqrt(rank ** skew) + 1 for rank in range(1, amount + 1)]
    largest = reach if full else min(reach, max(-(-total // amount), total * portions[0] // sum(portions)))
    least = 1 if total - largest >= amount - 1 else 0
    counts, rest = [largest] + [least] * (amount - 1), total - largest - least * (amount - 1)
    while rest > 0:
        candidates = [i for i in range(1, amount) if counts[i] < largest] or [i for i in range(1, amount) if counts[i] < reach]
        mass, remaining = sum([portions[i] for i in candidates]), rest
        for i in candidates:
            addition = min(reach - counts[i], max(1, remaining * portions[i] // mass), rest)
            counts[i] = counts[i] + addition
            rest = rest - addition
    return np.array(counts)


def setup_inputs(seed: int = 0) -> dict:
    arg_keys = jax.random.split(jax.random.key(seed), 9)
    bin_points = draw_bin_points(jax.random.fold_in(arg_keys[8], 71), 0)
    bin_plan_keys = jax.random.split(jax.random.fold_in(arg_keys[1], 1), BINS // BINS_DEV)
    bin_plan_turns = jax.random.permutation(jax.random.fold_in(arg_keys[1], 3), BINS // BINS_DEV)
    bin_plan = jax.vmap(lambda own, number: routed_block(jax.random.fold_in(arg_keys[1], 2), own, number, BINS_DEV, N_SFC, 1, CAP, 2))(bin_plan_keys, bin_plan_turns).reshape((BINS, 1))
    bin_leaf = set_ends(jax.random.randint(arg_keys[2], (BINS,), 0, LEAF_DEV), jax.random.fold_in(arg_keys[2], 1), 0, LEAF_DEV - 1).astype(jnp.int32)
    leaf_slots = jax.vmap(lambda own: jax.random.permutation(own, PAR1))(jax.random.split(arg_keys[3], N_SFC * 8)).reshape((N_SFC, 8, PAR1)).astype(jnp.int32)
    box_slots = jax.vmap(lambda own: jax.random.permutation(own, PAR2))(jax.random.split(arg_keys[4], N_SFC * 8)).reshape((N_SFC, 8, PAR2)).astype(jnp.int32)
    parent_cone = set_ends(jax.random.randint(arg_keys[5], (N_SFC, PAR1), 0, CONES), jax.random.fold_in(arg_keys[5], 1), 0, CONES - 1).astype(jnp.int32)
    box_cone = set_ends(jax.random.randint(arg_keys[6], (N_SFC, PAR2), 0, CONES), jax.random.fold_in(arg_keys[6], 1), 0, CONES - 1).astype(jnp.int32)
    cone_angles = jnp.clip(jax.random.uniform(arg_keys[7], (CONES, 2), jnp.float32, -3.140625, 3.140625), -3.140625, 3.140625)
    return {"bin_points": bin_points, "bin_plan": bin_plan, "bin_leaf": bin_leaf, "leaf_slots": leaf_slots, "box_slots": box_slots, "parent_cone": parent_cone, "box_cone": box_cone, "cone_angles": cone_angles}


kappa_leaf = 2.0
kappa_box = 4.0


def cheb_nodes():
    return np.cos((2.0 * np.arange(8) + 1.0) * np.pi / 16.0)


def lagrange(values):
    nodes = cheb_nodes()
    rows = []
    for center in range(8):
        weight = jnp.ones_like(values)
        for other in range(8):
            if other != center:
                weight = weight * ((values - float(nodes[other])) / float(nodes[center] - nodes[other]))
        rows.append(weight)
    return jnp.stack(rows, axis=-2)


def bin_expansions(points):
    count = points.shape[0]
    width = points.shape[2]
    basis = lagrange(points[:, 0:3])
    weighted = (points[:, 3:5, None, :] * basis[:, 0][:, None]).astype(jnp.bfloat16).reshape(count, 16, width)
    pair = (basis[:, 1][:, :, None, :] * basis[:, 2][:, None, :, :]).astype(jnp.bfloat16).reshape(count, 64, width)
    result = jnp.einsum("bcp,bqp->bcq", weighted.astype(jnp.float32), pair.astype(jnp.float32))
    return result.reshape(count, 2, 512)


def child_axes(octant):
    bits = [octant // 4, (octant // 2) % 2, octant % 2]
    nodes = cheb_nodes()
    return np.stack([0.5 * (2 * bit - 1) + 0.5 * nodes for bit in bits])


def child_matrix(octant):
    axes = child_axes(octant)
    first = lagrange(jnp.asarray(axes[0]).astype(jnp.float32))
    second = lagrange(jnp.asarray(axes[1]).astype(jnp.float32))
    third = lagrange(jnp.asarray(axes[2]).astype(jnp.float32))
    return jnp.einsum("ad,be,cf->abcdef", first, second, third).reshape(512, 512)


def node_phase(dirs, kappa, axes):
    first = jnp.asarray(axes[0]).astype(jnp.float32)
    second = jnp.asarray(axes[1]).astype(jnp.float32)
    third = jnp.asarray(axes[2]).astype(jnp.float32)
    angle = (dirs[:, 0, None, None, None] * first[None, :, None, None]
             + dirs[:, 1, None, None, None] * second[None, None, :, None]
             + dirs[:, 2, None, None, None] * third[None, None, None, :])
    angle = kappa * angle.reshape(dirs.shape[0], 512)
    return jnp.cos(angle), jnp.sin(angle)


def rotate(field, cosine, sine):
    real_part = field[:, 0]
    imag_part = field[:, 1]
    return jnp.stack([real_part * cosine - imag_part * sine, real_part * sine + imag_part * cosine], axis=1)


def cone_vectors(cone_angles):
    azimuth = cone_angles[:, 0]
    polar = cone_angles[:, 1]
    return jnp.stack([jnp.cos(azimuth) * jnp.sin(polar), jnp.sin(azimuth) * jnp.sin(polar), jnp.cos(polar)], axis=1)


def level_term(children, dirs, octant, kappa):
    cosine, sine = node_phase(dirs, kappa, child_axes(octant))
    turned = rotate(children, cosine, sine)
    matrix = child_matrix(octant)
    moved = jnp.dot(turned.reshape(-1, 512), matrix.T, preferred_element_type=jnp.float32, precision=lax.Precision.HIGHEST)
    return moved.reshape(children.shape[0], 2, 512)


def parent_turn(field, dirs, kappa):
    nodes = cheb_nodes()
    cosine, sine = node_phase(dirs, -kappa, np.stack([nodes, nodes, nodes]))
    return rotate(field, cosine, sine)


def level(children, slots, cones, directions, kappa, count):
    segments = children.shape[0]
    total = jnp.zeros((segments, count, 2, 512), jnp.float32)
    parent_dirs = directions[cones]
    seg_index = jnp.arange(segments, dtype=jnp.int32)[:, None]
    for octant in range(8):
        rows = children[:, octant::8]
        parents = slots[:, octant, :]
        child_dirs = jnp.take_along_axis(parent_dirs, parents[:, :, None], axis=1)
        term = level_term(rows.reshape(-1, 2, 512), child_dirs.reshape(-1, 3), octant, kappa)
        total = total.at[seg_index, parents].add(term.reshape(segments, count, 2, 512))
    turned = parent_turn(total.reshape(-1, 2, 512), parent_dirs.reshape(-1, 3), kappa)
    return turned.reshape(segments, count, 2, 512)


def reference(bin_points, bin_plan, bin_leaf, leaf_slots, box_slots, parent_cone, box_cone, cone_angles):
    total = bin_points.shape[0]
    width = bin_points.shape[2]
    block = math.gcd(total, 128)
    terms = lax.map(bin_expansions, bin_points.reshape(total // block, block, 5, width)).reshape(total, 2, 512)
    device = jnp.arange(total, dtype=jnp.int32) // BINS_DEV
    group = device % N_GRP
    leaf_index = (bin_plan[:, 0] * N_GRP + group) * LEAF_DEV + bin_leaf
    leaves = jax.ops.segment_sum(terms, leaf_index, num_segments=N_SFC * N_GRP * LEAF_DEV)
    directions = cone_vectors(cone_angles)
    children = leaves.reshape(N_SFC, N_GRP * LEAF_DEV, 2, 512)
    first_level = level(children, leaf_slots, parent_cone, directions, kappa_leaf, PAR1)
    second_level = level(first_level, box_slots, box_cone, directions, kappa_box, PAR2)
    return leaves, first_level.reshape(-1, 2, 512), second_level.reshape(-1, 2, 512)
```

```python
import functools

import jax
import jax.numpy as jnp
import ml_dtypes
import numpy as np
from jax import lax
from jax.experimental import pallas as pl
from jax.experimental.pallas import tpu as pltpu
from jax.sharding import PartitionSpec as P

kappa_leaf = 2.0
kappa_box = 4.0


def cheb_nodes():
    return np.cos((2.0 * np.arange(8) + 1.0) * np.pi / 16.0)


def lagrange_np(values):
    nodes = cheb_nodes()
    rows = []
    for center in range(8):
        weight = np.ones_like(values)
        for other in range(8):
            if other != center:
                weight = weight * (values - nodes[other]) / (nodes[center] - nodes[other])
        rows.append(weight)
    return np.stack(rows, axis=-2)


def child_axes(octant):
    bits = [octant // 4, octant // 2 % 2, octant % 2]
    nodes = cheb_nodes()
    return np.stack([0.5 * (2 * bit - 1) + 0.5 * nodes for bit in bits])


def child_matrices():
    rows = []
    for octant in range(8):
        first, second, third = [lagrange_np(axis) for axis in child_axes(octant)]
        rows.append(np.einsum("ad,be,cf->abcdef", first, second, third).reshape(512, 512))
    return np.stack(rows)


def basis_constants(width):
    nodes = cheb_nodes()
    rows = np.zeros((5, 8, width))
    for center in range(8):
        pair = min(center, 7 - center)
        others = [nodes[j] ** 2 for j in range(4) if j != pair]
        scale = 2.0 * nodes[center]
        for value in others:
            scale = scale * (nodes[center] ** 2 - value)
        for j in range(3):
            rows[j, center] = others[j]
        rows[3, center] = 1.0 / scale
        rows[4, center] = nodes[center] / scale
    return rows.astype(np.float32)


def octant_tables():
    positions = np.stack([child_axes(octant) for octant in range(8)])
    shape = (8, 8, 8, 8)
    grid = np.stack(
        [
            np.broadcast_to(positions[:, 0][:, :, None, None], shape),
            np.broadcast_to(positions[:, 1][:, None, :, None], shape),
            np.broadcast_to(positions[:, 2][:, None, None, :], shape),
        ],
        axis=1,
    )
    return grid.reshape(8, 3, 512).astype(np.float32)


def node_table():
    nodes = cheb_nodes()
    shape = (8, 8, 8)
    grid = np.stack(
        [
            np.broadcast_to(nodes[:, None, None], shape),
            np.broadcast_to(nodes[None, :, None], shape),
            np.broadcast_to(nodes[None, None, :], shape),
        ]
    )
    return grid.reshape(3, 512).astype(np.float32)


def term_kernel(block, unroll, index_ref, const_ref, point_ref, out_ref):
    step = pl.program_id(0)
    width = point_ref.shape[2]

    @pl.when(step == 0)
    def _():
        def clear(i, carry):
            out_ref[pl.ds(pl.multiple_of(i * 8, 8), 8)] = jnp.zeros((8, 8, 128), jnp.float32)
            return carry

        lax.fori_loop(0, out_ref.shape[0] // 8, clear, 0)

    tau = [const_ref[j] for j in range(5)]
    low = lax.broadcasted_iota(jnp.int32, (8, 128), 1) < 64

    def basis(row):
        row = jnp.broadcast_to(row, (8, width))
        square = row * row
        value = (square - tau[0]) * (square - tau[1]) * (square - tau[2])
        return value * (row * tau[3] + tau[4])

    def factors(i):
        first = basis(point_ref[i, 0:1, :])
        second = basis(point_ref[i, 1:2, :])
        third = basis(point_ref[i, 2:3, :])
        weighted = jnp.concatenate(
            [point_ref[i, 3:4, :] * first, point_ref[i, 4:5, :] * first], axis=0
        ).astype(jnp.bfloat16)
        pair = jnp.concatenate(
            [second[b : b + 1, :] * third for b in range(8)], axis=0
        ).astype(jnp.bfloat16)
        return weighted, pair

    def body(j, carry):
        values = []
        for k in range(unroll):
            i = j * 2 * unroll + 2 * k
            wa, pa = factors(i)
            wb, pb = factors(i + 1)
            result = lax.dot_general(
                jnp.concatenate([wa, wb], axis=0),
                jnp.concatenate([pa, pb], axis=0),
                (((1,), (1,)), ((), ())),
                preferred_element_type=jnp.float32,
            )
            one = jnp.where(low, result[0:8], pltpu.roll(result[8:16], 64, 1))
            two = jnp.where(low, pltpu.roll(result[16:24], 64, 1), result[24:32])
            values.append((i, one))
            values.append((i + 1, two))
        for i, value in values:
            spot = index_ref[step * block + i]
            out_ref[spot] += value
        return carry

    lax.fori_loop(0, block // (2 * unroll), body, 0)


def dense_terms(points, index, rows):
    count, _, width = points.shape
    block = 64
    return pl.pallas_call(
        functools.partial(term_kernel, block, 4),
        out_shape=jax.ShapeDtypeStruct((rows, 8, 128), jnp.float32),
        grid_spec=pltpu.PrefetchScalarGridSpec(
            num_scalar_prefetch=1,
            grid=(count // block,),
            in_specs=[
                pl.BlockSpec((5, 8, width), lambda i, index: (0, 0, 0)),
                pl.BlockSpec((block, 5, width), lambda i, index: (i, 0, 0)),
            ],
            out_specs=pl.BlockSpec((rows, 8, 128), lambda i, index: (0, 0, 0)),
        ),
        compiler_params=pltpu.CompilerParams(vmem_limit_bytes=48 * 1024 * 1024),
        name="bin_terms",
    )(index, jnp.asarray(basis_constants(width)), points)


def rotate(field, cosine, sine):
    real_part = field[:, 0]
    imag_part = field[:, 1]
    return jnp.stack(
        [real_part * cosine - imag_part * sine, real_part * sine + imag_part * cosine], axis=1
    )


def cone_vectors(cone_angles):
    azimuth = cone_angles[:, 0]
    polar = cone_angles[:, 1]
    return jnp.stack(
        [jnp.cos(azimuth) * jnp.sin(polar), jnp.sin(azimuth) * jnp.sin(polar), jnp.cos(polar)],
        axis=1,
    )


def look_up(table, index):
    onehot = (index[:, None] == jnp.arange(table.shape[0], dtype=jnp.int32)[None, :]).astype(
        jnp.float32
    )
    return jnp.dot(
        onehot, table, preferred_element_type=jnp.float32, precision=lax.Precision.HIGHEST
    )


def parent_turn(field, dirs, kappa):
    grid = jnp.asarray(node_table())
    angle = -kappa * (
        dirs[:, 0, None] * grid[0] + dirs[:, 1, None] * grid[1] + dirs[:, 2, None] * grid[2]
    )
    return rotate(field, jnp.cos(angle), jnp.sin(angle))


def split(values):
    high = values.astype(jnp.bfloat16)
    return high, (values - high.astype(jnp.float32)).astype(jnp.bfloat16)


def level_partial(children, slots, parent_dirs, kappa, matrices):
    count = children.shape[0]
    owners = parent_dirs.shape[0]
    parents = jnp.transpose(slots).reshape(count)
    match = jnp.arange(owners, dtype=jnp.int32)[:, None] == parents[None, :]
    child_dirs = jnp.dot(
        jnp.transpose(match.astype(jnp.float32)),
        parent_dirs,
        preferred_element_type=jnp.float32,
        precision=lax.Precision.HIGHEST,
    )
    grid = jnp.asarray(octant_tables())
    grouped = child_dirs.reshape(count // 8, 8, 3)
    angle = (
        grouped[:, :, 0, None] * grid[None, :, 0]
        + grouped[:, :, 1, None] * grid[None, :, 1]
        + grouped[:, :, 2, None] * grid[None, :, 2]
    )
    angle = kappa * angle.reshape(count, 512)
    turned = rotate(children, jnp.cos(angle), jnp.sin(angle))
    moved = jnp.einsum(
        "jopn,omn->jopm",
        turned.reshape(count // 8, 8, 2, 512).astype(jnp.bfloat16),
        matrices,
        preferred_element_type=jnp.float32,
    )
    picks = match.astype(jnp.bfloat16)
    high, low = split(moved.reshape(count, 1024))
    total = jnp.dot(picks, high, preferred_element_type=jnp.float32) + jnp.dot(
        picks, low, preferred_element_type=jnp.float32
    )
    return total.reshape(owners, 2, 512)


def per_device(
    bin_points, bin_plan, bin_leaf, leaf_slots, box_slots, parent_cone, box_cone, cone_angles
):
    peers = lax.axis_size("sfc")
    groups = lax.axis_size("grp")
    group_rank = lax.axis_index("grp")
    leaf_count = leaf_slots.shape[2] * 8
    index = bin_plan[:, 0] * leaf_count + bin_leaf
    dense = dense_terms(bin_points, index, peers * leaf_count)
    own = lax.psum_scatter(dense, "sfc", scatter_dimension=0, tiled=True)
    leaves = jnp.transpose(own.reshape(leaf_count, 8, 2, 64), (0, 2, 1, 3)).reshape(
        leaf_count, 2, 512
    )
    matrices = jnp.asarray(child_matrices().astype(ml_dtypes.bfloat16))
    directions = cone_vectors(cone_angles)
    parent_dirs = look_up(directions, parent_cone[0])
    upper_dirs = look_up(directions, box_cone[0])
    first_owned = parent_dirs.shape[0] // groups
    second_owned = upper_dirs.shape[0] // groups
    partial_value = level_partial(leaves, leaf_slots[0], parent_dirs, kappa_leaf, matrices)
    summed = lax.psum_scatter(partial_value, "grp", scatter_dimension=0, tiled=True)
    mine = lax.dynamic_slice_in_dim(parent_dirs, group_rank * first_owned, first_owned, 0)
    first_level = parent_turn(summed, mine, kappa_leaf)
    slots_mine = lax.dynamic_slice_in_dim(
        box_slots[0], group_rank * (first_owned // 8), first_owned // 8, 1
    )
    upper = level_partial(first_level, slots_mine, upper_dirs, kappa_box, matrices)
    upper_owned = lax.psum_scatter(upper, "grp", scatter_dimension=0, tiled=True)
    upper_mine = lax.dynamic_slice_in_dim(upper_dirs, group_rank * second_owned, second_owned, 0)
    second_level = parent_turn(upper_owned, upper_mine, kappa_box)
    return (leaves, first_level, second_level)


def solution(mesh):
    placed = (
        P(("sfc", "grp"), None, None),
        P(("sfc", "grp"), None),
        P(("sfc", "grp")),
        P("sfc", None, "grp"),
        P("sfc", None, None),
        P("sfc", None),
        P("sfc", None),
        P(),
    )
    return jax.shard_map(
        per_device,
        mesh=mesh,
        in_specs=placed,
        out_specs=(
            P(("sfc", "grp"), None, None),
            P(("sfc", "grp"), None, None),
            P(("sfc", "grp"), None, None),
        ),
        check_vma=False,
    )
```

```python
import functools

import jax
import jax.numpy as jnp
import ml_dtypes
import numpy as np
from jax import lax
from jax.experimental import pallas as pl
from jax.experimental.pallas import tpu as pltpu
from jax.sharding import PartitionSpec as P

kappa_leaf = 2.0
kappa_box = 4.0


def cheb_nodes():
    return np.cos((2.0 * np.arange(8) + 1.0) * np.pi / 16.0)


def lagrange_np(values):
    nodes = cheb_nodes()
    rows = []
    for center in range(8):
        weight = np.ones_like(values)
        for other in range(8):
            if other != center:
                weight = weight * (values - nodes[other]) / (nodes[center] - nodes[other])
        rows.append(weight)
    return np.stack(rows, axis=-2)


def child_axes(octant):
    bits = [octant // 4, octant // 2 % 2, octant % 2]
    nodes = cheb_nodes()
    return np.stack([0.5 * (2 * bit - 1) + 0.5 * nodes for bit in bits])


def child_matrices():
    rows = []
    for octant in range(8):
        first, second, third = [lagrange_np(axis) for axis in child_axes(octant)]
        rows.append(np.einsum("ad,be,cf->abcdef", first, second, third).reshape(512, 512))
    return np.stack(rows)


def basis_constants(width):
    nodes = cheb_nodes()
    rows = np.zeros((5, 8, width))
    for center in range(8):
        pair = min(center, 7 - center)
        others = [nodes[j] ** 2 for j in range(4) if j != pair]
        scale = 2.0 * nodes[center]
        for value in others:
            scale = scale * (nodes[center] ** 2 - value)
        for j in range(3):
            rows[j, center] = others[j]
        rows[3, center] = 1.0 / scale
        rows[4, center] = nodes[center] / scale
    return rows.astype(np.float32)


def octant_tables():
    positions = np.stack([child_axes(octant) for octant in range(8)])
    shape = (8, 8, 8, 8)
    grid = np.stack(
        [
            np.broadcast_to(positions[:, 0][:, :, None, None], shape),
            np.broadcast_to(positions[:, 1][:, None, :, None], shape),
            np.broadcast_to(positions[:, 2][:, None, None, :], shape),
        ],
        axis=1,
    )
    return grid.reshape(8, 3, 512).astype(np.float32)


def node_table():
    nodes = cheb_nodes()
    shape = (8, 8, 8)
    grid = np.stack(
        [
            np.broadcast_to(nodes[:, None, None], shape),
            np.broadcast_to(nodes[None, :, None], shape),
            np.broadcast_to(nodes[None, None, :], shape),
        ]
    )
    return grid.reshape(3, 512).astype(np.float32)


def term_kernel(block, unroll, index_ref, const_ref, point_ref, out_ref):
    step = pl.program_id(0)
    width = point_ref.shape[2]

    @pl.when(step == 0)
    def _():
        def clear(i, carry):
            out_ref[pl.ds(pl.multiple_of(i * 8, 8), 8)] = jnp.zeros((8, 8, 128), jnp.float32)
            return carry

        lax.fori_loop(0, out_ref.shape[0] // 8, clear, 0)

    tau = [const_ref[j] for j in range(5)]
    low = lax.broadcasted_iota(jnp.int32, (8, 128), 1) < 64

    def basis(row):
        row = jnp.broadcast_to(row, (8, width))
        square = row * row
        value = (square - tau[0]) * (square - tau[1]) * (square - tau[2])
        return value * (row * tau[3] + tau[4])

    def factors(rows, i):
        first = basis(rows[0, i : i + 1])
        second = basis(rows[1, i : i + 1])
        third = basis(rows[2, i : i + 1])
        weighted = jnp.concatenate(
            [rows[3, i : i + 1] * first, rows[4, i : i + 1] * first], axis=0
        ).astype(jnp.bfloat16)
        pair = jnp.concatenate(
            [second[b : b + 1] * third for b in range(8)], axis=0
        ).astype(jnp.bfloat16)
        return weighted, pair

    def body(j, carry):
        base = pl.multiple_of(j * 2 * unroll, 8)
        rows = point_ref[:, pl.ds(base, 2 * unroll), :]
        values = []
        for k in range(unroll):
            wa, pa = factors(rows, 2 * k)
            wb, pb = factors(rows, 2 * k + 1)
            result = lax.dot_general(
                jnp.concatenate([wa, wb], axis=0),
                jnp.concatenate([pa, pb], axis=0),
                (((1,), (1,)), ((), ())),
                preferred_element_type=jnp.float32,
            )
            values.append(jnp.where(low, result[0:8], pltpu.roll(result[8:16], 64, 1)))
            values.append(jnp.where(low, pltpu.roll(result[16:24], 64, 1), result[24:32]))
        for i, value in enumerate(values):
            out_ref[index_ref[step * block + base + i]] += value
        return carry

    lax.fori_loop(0, block // (2 * unroll), body, 0)


def dense_terms(points, index, rows):
    _, count, width = points.shape
    block = 128
    return pl.pallas_call(
        functools.partial(term_kernel, block, 16),
        out_shape=jax.ShapeDtypeStruct((rows, 8, 128), jnp.float32),
        grid_spec=pltpu.PrefetchScalarGridSpec(
            num_scalar_prefetch=1,
            grid=(count // block,),
            in_specs=[
                pl.BlockSpec((5, 8, width), lambda i, index: (0, 0, 0)),
                pl.BlockSpec((5, block, width), lambda i, index: (0, i, 0)),
            ],
            out_specs=pl.BlockSpec((rows, 8, 128), lambda i, index: (0, 0, 0)),
        ),
        compiler_params=pltpu.CompilerParams(vmem_limit_bytes=48 * 1024 * 1024),
        name="bin_terms",
    )(index, jnp.asarray(basis_constants(width)), points)


def greet(axis, targets):
    barrier = pltpu.get_barrier_semaphore()
    for target in targets:
        pl.semaphore_signal(
            barrier, inc=1, device_id={axis: target}, device_id_type=pl.DeviceIdType.MESH
        )
    pl.semaphore_wait(barrier, len(targets))


def halving_plan(n):
    depth = n.bit_length() - 1
    orders = [[0] + list(range(1, depth)), [0] + list(range(depth - 1, 0, -1))]
    plans = []
    for order in orders:
        stages = []
        for s, bit in enumerate(order):
            rest = order[s + 1 :]
            masks = [
                m
                for m in range(n)
                if (m >> bit) % 2 == 1 and all((m >> k) % 2 == 0 for k in order[:s])
            ]
            masks.sort(key=lambda m: tuple(-((m >> k) % 2) for k in rest))
            stages.append((bit, masks))
        plans.append(stages)
    return plans


def halving_kernel(axis, n, dense_ref, out_ref, kept, got, load_sem, send_sem, recv_sem):
    me = lax.axis_index(axis)
    depth = n.bit_length() - 1
    half = out_ref.shape[0] // 2
    bits = [(me // 2**k) % 2 for k in range(depth)]
    plans = halving_plan(n)
    partners = [me + 2**k * (1 - 2 * bits[k]) for k in range(depth)]
    greet(axis, partners)

    def block(mask):
        return sum(2**k * ((bits[k] + (mask >> k) % 2) % 2) for k in range(depth))

    slots = {}
    for h in range(2):
        for s, (bit, masks) in enumerate(plans[h]):
            for mask in masks:
                slots[(h, s, mask)] = len(slots)
    copies = {}

    def send(h, s, mask, source):
        slot = slots[(h, s, mask)]
        copy = pltpu.make_async_remote_copy(
            src_ref=source,
            dst_ref=got.at[slot],
            send_sem=send_sem.at[slot],
            recv_sem=recv_sem.at[slot],
            device_id={axis: partners[plans[h][s][0]]},
            device_id_type=pl.DeviceIdType.MESH,
        )
        copy.start()
        copies[(h, s, mask)] = copy

    for j in range(n // 2):
        for h in range(2):
            mask = plans[h][0][1][j]
            send(h, 0, mask, dense_ref.at[block(mask), pl.ds(h * half, half)])
    loads = {}
    for j in range(n // 2):
        for h in range(2):
            mask = plans[h][0][1][j] - 1
            load = pltpu.make_async_copy(
                dense_ref.at[block(mask), pl.ds(h * half, half)],
                kept.at[h, mask // 2],
                load_sem.at[h, mask // 2],
            )
            load.start()
            loads[(h, mask)] = load
    for s in range(depth):
        for j in range(n >> (s + 1)):
            for h in range(2):
                bit, masks = plans[h][s]
                mask = masks[j]
                goal = mask - 2**bit
                if s == 0:
                    loads[(h, goal)].wait()
                copies[(h, s, mask)].wait_recv()
                slot = slots[(h, s, mask)]

                def add(i, carry, h=h, goal=goal, slot=slot):
                    rows = pl.ds(pl.multiple_of(i * 8, 8), 8)
                    total = kept[h, goal // 2, rows] + got[slot, rows]
                    if goal == 0 and s == depth - 1:
                        out_ref[pl.ds(pl.multiple_of(h * half + i * 8, 8), 8)] = total
                    else:
                        kept[h, goal // 2, rows] = total
                    return carry

                lax.fori_loop(0, half // 8, add, 0)
                if goal and (goal >> plans[h][s + 1][0]) % 2 == 1:
                    send(h, s + 1, goal, kept.at[h, goal // 2])
    for copy in copies.values():
        copy.wait_send()


def halving_scatter(dense, axis, n, number):
    rows = dense.shape[1]
    tile = dense.shape[2:]
    half = rows // 2
    return pl.pallas_call(
        functools.partial(halving_kernel, axis, n),
        out_shape=jax.ShapeDtypeStruct((rows,) + tile, jnp.float32),
        in_specs=[pl.BlockSpec(memory_space=pl.ANY)],
        out_specs=pl.BlockSpec(memory_space=pltpu.VMEM),
        scratch_shapes=[
            pltpu.VMEM((2, n // 2, half) + tile, jnp.float32),
            pltpu.VMEM((2 * (n - 1), half) + tile, jnp.float32),
            pltpu.SemaphoreType.DMA((2, n // 2)),
            pltpu.SemaphoreType.DMA((2 * (n - 1),)),
            pltpu.SemaphoreType.DMA((2 * (n - 1),)),
        ],
        compiler_params=pltpu.CompilerParams(
            collective_id=number, has_side_effects=True, vmem_limit_bytes=48 * 1024 * 1024
        ),
        name="segment_sums",
    )(dense)


def direct_kernel(axis, n, part_ref, out_ref, got, send_sem, recv_sem):
    me = lax.axis_index(axis)
    targets = [lax.rem(me + d, n) for d in range(1, n)]
    greet(axis, targets)
    copies = []
    for d in range(n - 1):
        copy = pltpu.make_async_remote_copy(
            src_ref=part_ref.at[targets[d]],
            dst_ref=got.at[d],
            send_sem=send_sem.at[d],
            recv_sem=recv_sem.at[d],
            device_id={axis: targets[d]},
            device_id_type=pl.DeviceIdType.MESH,
        )
        copy.start()
        copies.append(copy)
    total = part_ref[me]
    for copy in copies:
        copy.wait_recv()
    for d in range(n - 1):
        total = total + got[d]
    out_ref[...] = total
    for copy in copies:
        copy.wait_send()


def direct_scatter(parts, axis, n, number):
    rows = parts.shape[0] // n
    width = parts.shape[1]
    return pl.pallas_call(
        functools.partial(direct_kernel, axis, n),
        out_shape=jax.ShapeDtypeStruct((rows, width), jnp.float32),
        in_specs=[pl.BlockSpec(memory_space=pltpu.VMEM)],
        out_specs=pl.BlockSpec(memory_space=pltpu.VMEM),
        scratch_shapes=[
            pltpu.VMEM((n - 1, rows, width), jnp.float32),
            pltpu.SemaphoreType.DMA((n - 1,)),
            pltpu.SemaphoreType.DMA((n - 1,)),
        ],
        compiler_params=pltpu.CompilerParams(
            collective_id=number, has_side_effects=True, vmem_limit_bytes=32 * 1024 * 1024
        ),
        name="group_sums",
    )(parts.reshape(n, rows, width))


def rotate(field, cosine, sine):
    real_part = field[:, 0]
    imag_part = field[:, 1]
    return jnp.stack(
        [real_part * cosine - imag_part * sine, real_part * sine + imag_part * cosine], axis=1
    )


def cone_vectors(cone_angles):
    azimuth = cone_angles[:, 0]
    polar = cone_angles[:, 1]
    return jnp.stack(
        [jnp.cos(azimuth) * jnp.sin(polar), jnp.sin(azimuth) * jnp.sin(polar), jnp.cos(polar)],
        axis=1,
    )


def look_up(table, index):
    onehot = (index[:, None] == jnp.arange(table.shape[0], dtype=jnp.int32)[None, :]).astype(
        jnp.float32
    )
    return jnp.dot(
        onehot, table, preferred_element_type=jnp.float32, precision=lax.Precision.HIGHEST
    )


def parent_turn(field, dirs, kappa):
    grid = jnp.asarray(node_table())
    angle = -kappa * (
        dirs[:, 0, None] * grid[0] + dirs[:, 1, None] * grid[1] + dirs[:, 2, None] * grid[2]
    )
    return rotate(field, jnp.cos(angle), jnp.sin(angle))


def split(values):
    high = values.astype(jnp.bfloat16)
    return high, (values - high.astype(jnp.float32)).astype(jnp.bfloat16)


def level_partial(children, slots, parent_dirs, kappa, matrices):
    count = children.shape[0]
    owners = parent_dirs.shape[0]
    parents = jnp.transpose(slots).reshape(count)
    match = jnp.arange(owners, dtype=jnp.int32)[:, None] == parents[None, :]
    child_dirs = jnp.dot(
        jnp.transpose(match.astype(jnp.float32)),
        parent_dirs,
        preferred_element_type=jnp.float32,
        precision=lax.Precision.HIGHEST,
    )
    grid = jnp.asarray(octant_tables())
    grouped = child_dirs.reshape(count // 8, 8, 3)
    angle = (
        grouped[:, :, 0, None] * grid[None, :, 0]
        + grouped[:, :, 1, None] * grid[None, :, 1]
        + grouped[:, :, 2, None] * grid[None, :, 2]
    )
    angle = kappa * angle.reshape(count, 512)
    turned = rotate(children, jnp.cos(angle), jnp.sin(angle))
    moved = sum(
        jnp.einsum("jopn,omn->jopm", value, matrix, preferred_element_type=jnp.float32)
        for value, matrix in zip(
            split(turned.reshape(count // 8, 8, 2, 512)) + split(turned.reshape(count // 8, 8, 2, 512))[:1],
            (matrices[0], matrices[0], matrices[1]),
        )
    )
    picks = match.astype(jnp.bfloat16)
    high, low = split(moved.reshape(count, 1024))
    total = jnp.dot(picks, high, preferred_element_type=jnp.float32) + jnp.dot(
        picks, low, preferred_element_type=jnp.float32
    )
    return total


def per_device(
    bin_points, bin_plan, bin_leaf, leaf_slots, box_slots, parent_cone, box_cone, cone_angles
):
    peers = lax.axis_size("sfc")
    groups = lax.axis_size("grp")
    group_rank = lax.axis_index("grp")
    leaf_count = leaf_slots.shape[2] * 8
    index = bin_plan[:, 0] * leaf_count + bin_leaf
    dense = dense_terms(jnp.transpose(bin_points, (1, 0, 2)), index, peers * leaf_count)
    own = halving_scatter(dense.reshape(peers, leaf_count, 8, 128), "sfc", peers, 0)
    leaves = jnp.transpose(own.reshape(leaf_count, 8, 2, 64), (0, 2, 1, 3)).reshape(
        leaf_count, 2, 512
    )
    exact = child_matrices()
    rounded = exact.astype(ml_dtypes.bfloat16)
    rest = (exact - rounded.astype(np.float64)).astype(ml_dtypes.bfloat16)
    matrices = (jnp.asarray(rounded), jnp.asarray(rest))
    directions = cone_vectors(cone_angles)
    parent_dirs = look_up(directions, parent_cone[0])
    upper_dirs = look_up(directions, box_cone[0])
    first_owned = parent_dirs.shape[0] // groups
    second_owned = upper_dirs.shape[0] // groups
    partial_value = level_partial(leaves, leaf_slots[0], parent_dirs, kappa_leaf, matrices)
    summed = direct_scatter(partial_value, "grp", groups, 1).reshape(first_owned, 2, 512)
    mine = lax.dynamic_slice_in_dim(parent_dirs, group_rank * first_owned, first_owned, 0)
    first_level = parent_turn(summed, mine, kappa_leaf)
    slots_mine = lax.dynamic_slice_in_dim(
        box_slots[0], group_rank * (first_owned // 8), first_owned // 8, 1
    )
    upper = level_partial(first_level, slots_mine, upper_dirs, kappa_box, matrices)
    upper_owned = direct_scatter(upper, "grp", groups, 2).reshape(second_owned, 2, 512)
    upper_mine = lax.dynamic_slice_in_dim(upper_dirs, group_rank * second_owned, second_owned, 0)
    second_level = parent_turn(upper_owned, upper_mine, kappa_box)
    return (leaves, first_level, second_level)


def solution(mesh):
    placed = (
        P(("sfc", "grp"), None, None),
        P(("sfc", "grp"), None),
        P(("sfc", "grp")),
        P("sfc", None, "grp"),
        P("sfc", None, None),
        P("sfc", None),
        P("sfc", None),
        P(),
    )
    return jax.shard_map(
        per_device,
        mesh=mesh,
        in_specs=placed,
        out_specs=(
            P(("sfc", "grp"), None, None),
            P(("sfc", "grp"), None, None),
            P(("sfc", "grp"), None, None),
        ),
        check_vma=False,
    )
```

```python
import functools

import jax
import jax.numpy as jnp
import ml_dtypes
import numpy as np
from jax import lax
from jax.experimental import pallas as pl
from jax.experimental.pallas import tpu as pltpu
from jax.sharding import PartitionSpec as P

kappa_leaf = 2.0
kappa_box = 4.0


def cheb_nodes():
    return np.cos((2.0 * np.arange(8) + 1.0) * np.pi / 16.0)


def lagrange_np(values):
    nodes = cheb_nodes()
    rows = []
    for center in range(8):
        weight = np.ones_like(values)
        for other in range(8):
            if other != center:
                weight = weight * (values - nodes[other]) / (nodes[center] - nodes[other])
        rows.append(weight)
    return np.stack(rows, axis=-2)


def child_axes(octant):
    bits = [octant // 4, octant // 2 % 2, octant % 2]
    nodes = cheb_nodes()
    return np.stack([0.5 * (2 * bit - 1) + 0.5 * nodes for bit in bits])


def child_matrices():
    rows = []
    for octant in range(8):
        first, second, third = [lagrange_np(axis) for axis in child_axes(octant)]
        rows.append(np.einsum("ad,be,cf->abcdef", first, second, third).reshape(512, 512))
    return np.stack(rows)


def basis_constants(width):
    nodes = cheb_nodes()
    rows = np.zeros((5, 8, width))
    for center in range(8):
        pair = min(center, 7 - center)
        others = [nodes[j] ** 2 for j in range(4) if j != pair]
        scale = 2.0 * nodes[center]
        for value in others:
            scale = scale * (nodes[center] ** 2 - value)
        for j in range(3):
            rows[j, center] = others[j]
        rows[3, center] = 1.0 / scale
        rows[4, center] = nodes[center] / scale
    even = np.array([0, 2, 4, 6, 0, 2, 4, 6])
    return np.concatenate([rows, rows[:, even], rows[:, even + 1]]).astype(np.float32)


def octant_tables():
    positions = np.stack([child_axes(octant) for octant in range(8)])
    shape = (8, 8, 8, 8)
    grid = np.stack(
        [
            np.broadcast_to(positions[:, 0][:, :, None, None], shape),
            np.broadcast_to(positions[:, 1][:, None, :, None], shape),
            np.broadcast_to(positions[:, 2][:, None, None, :], shape),
        ],
        axis=1,
    )
    return grid.reshape(8, 3, 512).astype(np.float32)


def node_table():
    nodes = cheb_nodes()
    shape = (8, 8, 8)
    grid = np.stack(
        [
            np.broadcast_to(nodes[:, None, None], shape),
            np.broadcast_to(nodes[None, :, None], shape),
            np.broadcast_to(nodes[None, None, :], shape),
        ]
    )
    return grid.reshape(3, 512).astype(np.float32)


def greet(axis, targets):
    barrier = pltpu.get_barrier_semaphore()
    for target in targets:
        pl.semaphore_signal(
            barrier, inc=1, device_id={axis: target}, device_id_type=pl.DeviceIdType.MESH
        )
    pl.semaphore_wait(barrier, len(targets))


def halving_plan(n):
    depth = n.bit_length() - 1
    orders = [[0] + list(range(1, depth)), [0] + list(range(depth - 1, 0, -1))]
    plans = []
    for order in orders:
        stages = []
        for s, bit in enumerate(order):
            rest = order[s + 1 :]
            masks = [
                m
                for m in range(n)
                if (m >> bit) % 2 == 1 and all((m >> k) % 2 == 0 for k in order[:s])
            ]
            masks.sort(key=lambda m: tuple(-((m >> k) % 2) for k in rest))
            stages.append((bit, masks))
        plans.append(stages)
    return plans


def migrate_kernel(
    axis,
    n,
    unroll,
    order_ref,
    const_ref,
    label_ref,
    point_ref,
    out_ref,
    terms,
    work,
    near,
    far,
    near_send,
    near_recv,
    far_send,
    far_recv,
):
    me = lax.axis_index(axis)
    depth = n.bit_length() - 1
    width = point_ref.shape[2]
    rows = out_ref.shape[0]
    half = rows // 2
    capacity = label_ref.shape[2]
    bits = [(me // 2**k) % 2 for k in range(depth)]
    plans = halving_plan(n)
    partners = [me + 2**k * (1 - 2 * bits[k]) for k in range(depth)]
    greet(axis, partners)
    lane = lax.broadcasted_iota(jnp.int32, (8, 128), 1) < 64
    upper = lax.broadcasted_iota(jnp.int32, (8, width), 0) < 4

    def basis(row, kind):
        row = jnp.broadcast_to(row, (8, width))
        square = row * row
        tau = [const_ref[5 * kind + j] for j in range(5)]
        value = (square - tau[0]) * (square - tau[1]) * (square - tau[2])
        return value * (row * tau[3] + tau[4])

    def factors(spot):
        row = [point_ref[c, pl.ds(spot, 1), :] for c in range(5)]
        second = basis(row[1], 0)
        third = basis(row[2], 0)
        density = jnp.where(
            upper, jnp.broadcast_to(row[3], (8, width)), jnp.broadcast_to(row[4], (8, width))
        )
        weighted = jnp.concatenate(
            [density * basis(row[0], 1), density * basis(row[0], 2)], axis=0
        ).astype(jnp.bfloat16)
        pair = jnp.concatenate(
            [second[b : b + 1] * third for b in range(8)], axis=0
        ).astype(jnp.bfloat16)
        return weighted, pair

    def compute(mask):
        block = sum(2**k * ((bits[k] + (mask // 2**k) % 2) % 2) for k in range(depth))

        def bins(j, carry):
            base = j * 2 * unroll
            values = []
            for k in range(unroll):
                wa, pa = factors(order_ref[block * capacity + base + 2 * k])
                wb, pb = factors(order_ref[block * capacity + base + 2 * k + 1])
                result = lax.dot_general(
                    jnp.concatenate([wa, wb], axis=0),
                    jnp.concatenate([pa, pb], axis=0),
                    (((1,), (1,)), ((), ())),
                    preferred_element_type=jnp.float32,
                )
                values.append(jnp.where(lane, result[0:8], pltpu.roll(result[8:16], 64, 1)))
                values.append(jnp.where(lane, pltpu.roll(result[16:24], 64, 1), result[24:32]))
            for i, value in enumerate(values):
                terms[pl.ds(base + i, 8, stride=capacity), :] = value
            return carry

        lax.fori_loop(0, capacity // (2 * unroll), bins, 0)
        picks = (
            lax.broadcasted_iota(jnp.int32, (rows, capacity), 0) == label_ref[block]
        ).astype(jnp.float32).astype(jnp.bfloat16)
        picks = jnp.concatenate([picks, picks], axis=1)
        for pairing in range(4):
            parts = [
                terms[(2 * pairing + e) * capacity : (2 * pairing + e + 1) * capacity, :]
                for e in range(2)
            ]
            value = jnp.concatenate(parts, axis=1)
            high = value.astype(jnp.bfloat16)
            low = (value - high.astype(jnp.float32)).astype(jnp.bfloat16)
            work[mask, :, 256 * pairing : 256 * (pairing + 1)] = jnp.dot(
                picks, jnp.concatenate([high, low], axis=0), preferred_element_type=jnp.float32
            )

    def near_copy(h, pair):
        return pltpu.make_async_remote_copy(
            src_ref=work.at[2 * pair + 1, pl.ds(h * half, half)],
            dst_ref=near.at[h, pair],
            send_sem=near_send.at[h, pair],
            recv_sem=near_recv.at[h, pair],
            device_id={axis: partners[0]},
            device_id_type=pl.DeviceIdType.MESH,
        )

    slots = {}
    for h in range(2):
        for s in range(1, depth):
            for mask in plans[h][s][1]:
                slots[(h, s, mask)] = len(slots)

    def far_copy(h, s, mask):
        slot = slots[(h, s, mask)]
        return pltpu.make_async_remote_copy(
            src_ref=work.at[mask, pl.ds(h * half, half)],
            dst_ref=far.at[slot],
            send_sem=far_send.at[slot],
            recv_sem=far_recv.at[slot],
            device_id={axis: partners[plans[h][s][0]]},
            device_id_type=pl.DeviceIdType.MESH,
        )

    def add(mask, h, other, target=None):
        def step(i, carry):
            spot = pl.ds(pl.multiple_of(h * half + i * 8, 8), 8)
            total = work[mask, spot] + other[pl.ds(pl.multiple_of(i * 8, 8), 8)]
            if target is None:
                work[mask, spot] = total
            else:
                target[spot] = total
            return carry

        lax.fori_loop(0, half // 8, step, 0)

    def exchange(i, carry):
        pair = n // 2 - 1 - i

        def one(r, carry):
            compute(2 * pair + 1 - r)

            @pl.when(r == 0)
            def _():
                for h in range(2):
                    near_copy(h, pair).start()

            return carry

        lax.fori_loop(0, 2, one, 0)
        for h in range(2):
            near_copy(h, pair).wait_recv()
            add(2 * pair, h, near.at[h, pair])
            if depth > 1:
                for mask in plans[h][1][1]:

                    @pl.when(2 * pair == mask)
                    def _(h=h, mask=mask):
                        far_copy(h, 1, mask).start()

        return carry

    lax.fori_loop(0, n // 2, exchange, 0)
    for s in range(1, depth):
        for j in range(n >> (s + 1)):
            for h in range(2):
                bit, masks = plans[h][s]
                goal = masks[j] - 2**bit
                far_copy(h, s, masks[j]).wait_recv()
                last = goal == 0 and s == depth - 1
                add(goal, h, far.at[slots[(h, s, masks[j])]], out_ref if last else None)
                if goal and (goal >> plans[h][s + 1][0]) % 2 == 1:
                    far_copy(h, s + 1, goal).start()
    for h in range(2):
        for pair in range(n // 2):
            near_copy(h, pair).wait_send()
    for h, s, mask in slots:
        far_copy(h, s, mask).wait_send()


def migrate(points, order, labels, axis, n, rows, number):
    width = points.shape[2]
    capacity = labels.shape[1]
    half = rows // 2
    later = 2 * (n - 1 - n // 2)
    vmem = pl.BlockSpec(memory_space=pltpu.VMEM)
    return pl.pallas_call(
        functools.partial(migrate_kernel, axis, n, 16),
        out_shape=jax.ShapeDtypeStruct((rows, 1024), jnp.float32),
        in_specs=[pl.BlockSpec(memory_space=pltpu.SMEM), vmem, vmem, vmem],
        out_specs=vmem,
        scratch_shapes=[
            pltpu.VMEM((8 * capacity, 128), jnp.float32),
            pltpu.VMEM((n, rows, 1024), jnp.float32),
            pltpu.VMEM((2, n // 2, half, 1024), jnp.float32),
            pltpu.VMEM((later, half, 1024), jnp.float32),
            pltpu.SemaphoreType.DMA((2, n // 2)),
            pltpu.SemaphoreType.DMA((2, n // 2)),
            pltpu.SemaphoreType.DMA((later,)),
            pltpu.SemaphoreType.DMA((later,)),
        ],
        compiler_params=pltpu.CompilerParams(
            collective_id=number, has_side_effects=True, vmem_limit_bytes=56 * 1024 * 1024
        ),
        name="migrate",
    )(order, jnp.asarray(basis_constants(width)), labels[:, None, :], points)


def direct_kernel(axis, n, part_ref, out_ref, got, send_sem, recv_sem):
    me = lax.axis_index(axis)
    targets = [lax.rem(me + d, n) for d in range(1, n)]
    greet(axis, targets)
    copies = []
    for d in range(n - 1):
        copy = pltpu.make_async_remote_copy(
            src_ref=part_ref.at[targets[d]],
            dst_ref=got.at[d],
            send_sem=send_sem.at[d],
            recv_sem=recv_sem.at[d],
            device_id={axis: targets[d]},
            device_id_type=pl.DeviceIdType.MESH,
        )
        copy.start()
        copies.append(copy)
    total = part_ref[me]
    for copy in copies:
        copy.wait_recv()
    for d in range(n - 1):
        total = total + got[d]
    out_ref[...] = total
    for copy in copies:
        copy.wait_send()


def direct_scatter(parts, axis, n, number):
    rows = parts.shape[0] // n
    width = parts.shape[1]
    return pl.pallas_call(
        functools.partial(direct_kernel, axis, n),
        out_shape=jax.ShapeDtypeStruct((rows, width), jnp.float32),
        in_specs=[pl.BlockSpec(memory_space=pltpu.VMEM)],
        out_specs=pl.BlockSpec(memory_space=pltpu.VMEM),
        scratch_shapes=[
            pltpu.VMEM((n - 1, rows, width), jnp.float32),
            pltpu.SemaphoreType.DMA((n - 1,)),
            pltpu.SemaphoreType.DMA((n - 1,)),
        ],
        compiler_params=pltpu.CompilerParams(
            collective_id=number, has_side_effects=True, vmem_limit_bytes=32 * 1024 * 1024
        ),
        name="group_sums",
    )(parts.reshape(n, rows, width))


def rotate(field, cosine, sine):
    real_part = field[:, 0]
    imag_part = field[:, 1]
    return jnp.stack(
        [real_part * cosine - imag_part * sine, real_part * sine + imag_part * cosine], axis=1
    )


def cone_vectors(cone_angles):
    azimuth = cone_angles[:, 0]
    polar = cone_angles[:, 1]
    return jnp.stack(
        [jnp.cos(azimuth) * jnp.sin(polar), jnp.sin(azimuth) * jnp.sin(polar), jnp.cos(polar)],
        axis=1,
    )


def look_up(table, index):
    onehot = (index[:, None] == jnp.arange(table.shape[0], dtype=jnp.int32)[None, :]).astype(
        jnp.float32
    )
    return jnp.dot(
        onehot, table, preferred_element_type=jnp.float32, precision=lax.Precision.HIGHEST
    )


def parent_turn(field, dirs, kappa):
    grid = jnp.asarray(node_table())
    angle = -kappa * (
        dirs[:, 0, None] * grid[0] + dirs[:, 1, None] * grid[1] + dirs[:, 2, None] * grid[2]
    )
    return rotate(field, jnp.cos(angle), jnp.sin(angle))


def split(values):
    high = lax.reduce_precision(values, 8, 7)
    return high.astype(jnp.bfloat16), (values - high).astype(jnp.bfloat16)


def level_partial(children, slots, parent_dirs, kappa, matrices):
    count = children.shape[0]
    owners = parent_dirs.shape[0]
    parents = jnp.transpose(slots).reshape(count)
    match = jnp.arange(owners, dtype=jnp.int32)[:, None] == parents[None, :]
    child_dirs = jnp.dot(
        jnp.transpose(match.astype(jnp.float32)),
        parent_dirs,
        preferred_element_type=jnp.float32,
        precision=lax.Precision.HIGHEST,
    )
    grid = jnp.asarray(octant_tables())
    grouped = child_dirs.reshape(count // 8, 8, 3)
    angle = (
        grouped[:, :, 0, None] * grid[None, :, 0]
        + grouped[:, :, 1, None] * grid[None, :, 1]
        + grouped[:, :, 2, None] * grid[None, :, 2]
    )
    angle = kappa * angle.reshape(count, 512)
    turned = rotate(children, jnp.cos(angle), jnp.sin(angle))
    moved = sum(
        jnp.einsum("jopn,omn->jopm", value, matrix, preferred_element_type=jnp.float32)
        for value, matrix in zip(
            split(turned.reshape(count // 8, 8, 2, 512)) + split(turned.reshape(count // 8, 8, 2, 512))[:1],
            (matrices[0], matrices[0], matrices[1]),
        )
    )
    picks = match.astype(jnp.bfloat16)
    high, low = split(moved.reshape(count, 1024))
    total = jnp.dot(picks, high, preferred_element_type=jnp.float32) + jnp.dot(
        picks, low, preferred_element_type=jnp.float32
    )
    return total


def per_device(
    bin_points, bin_plan, bin_leaf, leaf_slots, box_slots, parent_cone, box_cone, cone_angles
):
    peers = lax.axis_size("sfc")
    groups = lax.axis_size("grp")
    group_rank = lax.axis_index("grp")
    leaf_count = leaf_slots.shape[2] * 8
    count = bin_points.shape[0]
    capacity = count // 8
    target = bin_plan[:, 0]
    number = jnp.arange(count, dtype=jnp.int32)
    ahead = (target[:, None] == target[None, :]) & (number[None, :] < number[:, None])
    position = target * capacity + jnp.sum(ahead.astype(jnp.int32), axis=1)
    taken = jnp.arange(peers * capacity, dtype=jnp.int32)[:, None] == position[None, :]
    order = jnp.sum(jnp.where(taken, number[None, :], 0), axis=1)
    labels = jnp.sum(jnp.where(taken, bin_leaf[None, :] + 1, 0), axis=1) - 1
    leaves = migrate(
        jnp.transpose(bin_points, (1, 0, 2)),
        order,
        labels.reshape(peers, capacity),
        "sfc",
        peers,
        leaf_count,
        0,
    ).reshape(leaf_count, 2, 512)
    exact = child_matrices()
    rounded = exact.astype(ml_dtypes.bfloat16)
    rest = (exact - rounded.astype(np.float64)).astype(ml_dtypes.bfloat16)
    matrices = (jnp.asarray(rounded), jnp.asarray(rest))
    directions = cone_vectors(cone_angles)
    parent_dirs = look_up(directions, parent_cone[0])
    upper_dirs = look_up(directions, box_cone[0])
    first_owned = parent_dirs.shape[0] // groups
    second_owned = upper_dirs.shape[0] // groups
    partial_value = level_partial(leaves, leaf_slots[0], parent_dirs, kappa_leaf, matrices)
    summed = direct_scatter(partial_value, "grp", groups, 1).reshape(first_owned, 2, 512)
    mine = lax.dynamic_slice_in_dim(parent_dirs, group_rank * first_owned, first_owned, 0)
    first_level = parent_turn(summed, mine, kappa_leaf)
    slots_mine = lax.dynamic_slice_in_dim(
        box_slots[0], group_rank * (first_owned // 8), first_owned // 8, 1
    )
    upper = level_partial(first_level, slots_mine, upper_dirs, kappa_box, matrices)
    upper_owned = direct_scatter(upper, "grp", groups, 2).reshape(second_owned, 2, 512)
    upper_mine = lax.dynamic_slice_in_dim(upper_dirs, group_rank * second_owned, second_owned, 0)
    second_level = parent_turn(upper_owned, upper_mine, kappa_box)
    return (leaves, first_level, second_level)


def solution(mesh):
    placed = (
        P(("sfc", "grp"), None, None),
        P(("sfc", "grp"), None),
        P(("sfc", "grp")),
        P("sfc", None, "grp"),
        P("sfc", None, None),
        P("sfc", None),
        P("sfc", None),
        P(),
    )
    return jax.shard_map(
        per_device,
        mesh=mesh,
        in_specs=placed,
        out_specs=(
            P(("sfc", "grp"), None, None),
            P(("sfc", "grp"), None, None),
            P(("sfc", "grp"), None, None),
        ),
        check_vma=False,
    )
```

```python
import functools

import jax
import jax.numpy as jnp
import ml_dtypes
import numpy as np
from jax import lax
from jax.experimental import pallas as pl
from jax.experimental.pallas import tpu as pltpu
from jax.sharding import PartitionSpec as P

kappa_leaf = 2.0
kappa_box = 4.0


def cheb_nodes():
    return np.cos((2.0 * np.arange(8) + 1.0) * np.pi / 16.0)


def lagrange_np(values):
    nodes = cheb_nodes()
    rows = []
    for center in range(8):
        weight = np.ones_like(values)
        for other in range(8):
            if other != center:
                weight = weight * (values - nodes[other]) / (nodes[center] - nodes[other])
        rows.append(weight)
    return np.stack(rows, axis=-2)


def child_axes(octant):
    bits = [octant // 4, octant // 2 % 2, octant % 2]
    nodes = cheb_nodes()
    return np.stack([0.5 * (2 * bit - 1) + 0.5 * nodes for bit in bits])


def child_matrices():
    rows = []
    for octant in range(8):
        first, second, third = [lagrange_np(axis) for axis in child_axes(octant)]
        rows.append(np.einsum("ad,be,cf->abcdef", first, second, third).reshape(512, 512))
    return np.stack(rows)


def basis_constants(width):
    nodes = cheb_nodes()
    rows = np.zeros((5, 8, width))
    for center in range(8):
        pair = min(center, 7 - center)
        others = [nodes[j] ** 2 for j in range(4) if j != pair]
        scale = 2.0 * nodes[center]
        for value in others:
            scale = scale * (nodes[center] ** 2 - value)
        for j in range(3):
            rows[j, center] = others[j]
        rows[3, center] = 1.0 / scale
        rows[4, center] = nodes[center] / scale
    even = np.array([0, 2, 4, 6, 0, 2, 4, 6])
    return np.concatenate([rows, rows[:, even], rows[:, even + 1]]).astype(np.float32)


def octant_tables():
    positions = np.stack([child_axes(octant) for octant in range(8)])
    shape = (8, 8, 8, 8)
    grid = np.stack(
        [
            np.broadcast_to(positions[:, 0][:, :, None, None], shape),
            np.broadcast_to(positions[:, 1][:, None, :, None], shape),
            np.broadcast_to(positions[:, 2][:, None, None, :], shape),
        ],
        axis=1,
    )
    return grid.reshape(8, 3, 512).astype(np.float32)


def node_table():
    nodes = cheb_nodes()
    shape = (8, 8, 8)
    grid = np.stack(
        [
            np.broadcast_to(nodes[:, None, None], shape),
            np.broadcast_to(nodes[None, :, None], shape),
            np.broadcast_to(nodes[None, None, :], shape),
        ]
    )
    return grid.reshape(3, 512).astype(np.float32)


def greet(axis, targets):
    barrier = pltpu.get_barrier_semaphore()
    for target in targets:
        pl.semaphore_signal(
            barrier, inc=1, device_id={axis: target}, device_id_type=pl.DeviceIdType.MESH
        )
    pl.semaphore_wait(barrier, len(targets))


def halving_plan(n):
    depth = n.bit_length() - 1
    orders = [[0] + list(range(1, depth)), [0] + list(range(depth - 1, 0, -1))]
    plans = []
    for order in orders:
        stages = []
        for s, bit in enumerate(order):
            rest = order[s + 1 :]
            masks = [
                m
                for m in range(n)
                if (m >> bit) % 2 == 1 and all((m >> k) % 2 == 0 for k in order[:s])
            ]
            masks.sort(key=lambda m: tuple(-((m >> k) % 2) for k in rest))
            stages.append((bit, masks))
        plans.append(stages)
    return plans


def migrate_kernel(
    axis,
    n,
    unroll,
    order_ref,
    const_ref,
    label_ref,
    point_ref,
    out_ref,
    terms,
    work,
    near,
    far,
    near_send,
    near_recv,
    far_send,
    far_recv,
):
    me = lax.axis_index(axis)
    depth = n.bit_length() - 1
    width = point_ref.shape[2]
    rows = out_ref.shape[0]
    half = rows // 2
    capacity = label_ref.shape[2]
    bits = [(me // 2**k) % 2 for k in range(depth)]
    plans = halving_plan(n)
    partners = [me + 2**k * (1 - 2 * bits[k]) for k in range(depth)]
    greet(axis, partners)
    lane = lax.broadcasted_iota(jnp.int32, (8, 128), 1) < 64
    upper = lax.broadcasted_iota(jnp.int32, (8, width), 0) < 4

    def basis(row, kind):
        row = jnp.broadcast_to(row, (8, width))
        square = row * row
        tau = [const_ref[5 * kind + j] for j in range(5)]
        value = (square - tau[0]) * (square - tau[1]) * (square - tau[2])
        return value * (row * tau[3] + tau[4])

    def factors(spot):
        row = [point_ref[c, pl.ds(spot, 1), :] for c in range(5)]
        second = basis(row[1], 0)
        third = basis(row[2], 0)
        density = jnp.where(
            upper, jnp.broadcast_to(row[3], (8, width)), jnp.broadcast_to(row[4], (8, width))
        )
        weighted = jnp.concatenate(
            [density * basis(row[0], 1), density * basis(row[0], 2)], axis=0
        ).astype(jnp.bfloat16)
        pair = jnp.concatenate(
            [second[b : b + 1] * third for b in range(8)], axis=0
        ).astype(jnp.bfloat16)
        return weighted, pair

    def compute(mask):
        block = sum(2**k * ((bits[k] + (mask // 2**k) % 2) % 2) for k in range(depth))

        def bins(j, carry):
            base = j * 2 * unroll
            values = []
            for k in range(unroll):
                wa, pa = factors(order_ref[block * capacity + base + 2 * k])
                wb, pb = factors(order_ref[block * capacity + base + 2 * k + 1])
                result = lax.dot_general(
                    jnp.concatenate([wa, wb], axis=0),
                    jnp.concatenate([pa, pb], axis=0),
                    (((1,), (1,)), ((), ())),
                    preferred_element_type=jnp.float32,
                )
                values.append(jnp.where(lane, result[0:8], pltpu.roll(result[8:16], 64, 1)))
                values.append(jnp.where(lane, pltpu.roll(result[16:24], 64, 1), result[24:32]))
            for i, value in enumerate(values):
                terms[pl.ds(base + i, 8, stride=capacity), :] = value
            return carry

        lax.fori_loop(0, capacity // (2 * unroll), bins, 0)
        picks = (
            lax.broadcasted_iota(jnp.int32, (rows, capacity), 0) == label_ref[block]
        ).astype(jnp.float32).astype(jnp.bfloat16)
        picks = jnp.concatenate([picks, picks], axis=1)
        for pairing in range(4):
            parts = [
                terms[(2 * pairing + e) * capacity : (2 * pairing + e + 1) * capacity, :]
                for e in range(2)
            ]
            value = jnp.concatenate(parts, axis=1)
            high = value.astype(jnp.bfloat16)
            low = (value - high.astype(jnp.float32)).astype(jnp.bfloat16)
            work[mask, :, 256 * pairing : 256 * (pairing + 1)] = jnp.dot(
                picks, jnp.concatenate([high, low], axis=0), preferred_element_type=jnp.float32
            )

    def near_copy(h, pair):
        return pltpu.make_async_remote_copy(
            src_ref=work.at[2 * pair + 1, pl.ds(h * half, half)],
            dst_ref=near.at[h, pair],
            send_sem=near_send.at[h, pair],
            recv_sem=near_recv.at[h, pair],
            device_id={axis: partners[0]},
            device_id_type=pl.DeviceIdType.MESH,
        )

    slots = {}
    for h in range(2):
        for s in range(1, depth):
            for mask in plans[h][s][1]:
                slots[(h, s, mask)] = len(slots)

    def far_copy(h, s, mask):
        slot = slots[(h, s, mask)]
        return pltpu.make_async_remote_copy(
            src_ref=work.at[mask, pl.ds(h * half, half)],
            dst_ref=far.at[slot],
            send_sem=far_send.at[slot],
            recv_sem=far_recv.at[slot],
            device_id={axis: partners[plans[h][s][0]]},
            device_id_type=pl.DeviceIdType.MESH,
        )

    def add(mask, h, other, target=None):
        def step(i, carry):
            spot = pl.ds(pl.multiple_of(h * half + i * 8, 8), 8)
            total = work[mask, spot] + other[pl.ds(pl.multiple_of(i * 8, 8), 8)]
            if target is None:
                work[mask, spot] = total
            else:
                target[spot] = total
            return carry

        lax.fori_loop(0, half // 8, step, 0)

    def exchange(i, carry):
        pair = n // 2 - 1 - i

        def one(r, carry):
            compute(2 * pair + 1 - r)

            @pl.when(r == 0)
            def _():
                for h in range(2):
                    near_copy(h, pair).start()

            return carry

        lax.fori_loop(0, 2, one, 0)
        for h in range(2):
            near_copy(h, pair).wait_recv()
            add(2 * pair, h, near.at[h, pair])
            if depth > 1:
                for mask in plans[h][1][1]:

                    @pl.when(2 * pair == mask)
                    def _(h=h, mask=mask):
                        far_copy(h, 1, mask).start()

        return carry

    lax.fori_loop(0, n // 2, exchange, 0)
    for s in range(1, depth):
        for j in range(n >> (s + 1)):
            for h in range(2):
                bit, masks = plans[h][s]
                goal = masks[j] - 2**bit
                far_copy(h, s, masks[j]).wait_recv()
                last = goal == 0 and s == depth - 1
                add(goal, h, far.at[slots[(h, s, masks[j])]], out_ref if last else None)
                if goal and (goal >> plans[h][s + 1][0]) % 2 == 1:
                    far_copy(h, s + 1, goal).start()
    for h in range(2):
        for pair in range(n // 2):
            near_copy(h, pair).wait_send()
    for h, s, mask in slots:
        far_copy(h, s, mask).wait_send()


def migrate(points, order, labels, axis, n, rows, number):
    width = points.shape[2]
    capacity = labels.shape[1]
    half = rows // 2
    later = 2 * (n - 1 - n // 2)
    vmem = pl.BlockSpec(memory_space=pltpu.VMEM)
    return pl.pallas_call(
        functools.partial(migrate_kernel, axis, n, 16),
        out_shape=jax.ShapeDtypeStruct((rows, 1024), jnp.float32),
        in_specs=[pl.BlockSpec(memory_space=pltpu.SMEM), vmem, vmem, vmem],
        out_specs=vmem,
        scratch_shapes=[
            pltpu.VMEM((8 * capacity, 128), jnp.float32),
            pltpu.VMEM((n, rows, 1024), jnp.float32),
            pltpu.VMEM((2, n // 2, half, 1024), jnp.float32),
            pltpu.VMEM((later, half, 1024), jnp.float32),
            pltpu.SemaphoreType.DMA((2, n // 2)),
            pltpu.SemaphoreType.DMA((2, n // 2)),
            pltpu.SemaphoreType.DMA((later,)),
            pltpu.SemaphoreType.DMA((later,)),
        ],
        compiler_params=pltpu.CompilerParams(
            collective_id=number, has_side_effects=True, vmem_limit_bytes=56 * 1024 * 1024
        ),
        name="migrate",
    )(order, jnp.asarray(basis_constants(width)), labels[:, None, :], points)


def direct_kernel(axis, n, part_ref, out_ref, got, send_sem, recv_sem):
    me = lax.axis_index(axis)
    targets = [lax.rem(me + d, n) for d in range(1, n)]
    greet(axis, targets)
    copies = []
    for d in range(n - 1):
        copy = pltpu.make_async_remote_copy(
            src_ref=part_ref.at[targets[d]],
            dst_ref=got.at[d],
            send_sem=send_sem.at[d],
            recv_sem=recv_sem.at[d],
            device_id={axis: targets[d]},
            device_id_type=pl.DeviceIdType.MESH,
        )
        copy.start()
        copies.append(copy)
    total = part_ref[me]
    for copy in copies:
        copy.wait_recv()
    for d in range(n - 1):
        total = total + got[d]
    out_ref[...] = total
    for copy in copies:
        copy.wait_send()


def direct_scatter(parts, axis, n, number):
    rows = parts.shape[0] // n
    width = parts.shape[1]
    return pl.pallas_call(
        functools.partial(direct_kernel, axis, n),
        out_shape=jax.ShapeDtypeStruct((rows, width), jnp.float32),
        in_specs=[pl.BlockSpec(memory_space=pltpu.VMEM)],
        out_specs=pl.BlockSpec(memory_space=pltpu.VMEM),
        scratch_shapes=[
            pltpu.VMEM((n - 1, rows, width), jnp.float32),
            pltpu.SemaphoreType.DMA((n - 1,)),
            pltpu.SemaphoreType.DMA((n - 1,)),
        ],
        compiler_params=pltpu.CompilerParams(
            collective_id=number, has_side_effects=True, vmem_limit_bytes=32 * 1024 * 1024
        ),
        name="group_sums",
    )(parts.reshape(n, rows, width))


def rotate(field, cosine, sine):
    real_part = field[:, 0]
    imag_part = field[:, 1]
    return jnp.stack(
        [real_part * cosine - imag_part * sine, real_part * sine + imag_part * cosine], axis=1
    )


def cone_vectors(cone_angles):
    azimuth = cone_angles[:, 0]
    polar = cone_angles[:, 1]
    return jnp.stack(
        [jnp.cos(azimuth) * jnp.sin(polar), jnp.sin(azimuth) * jnp.sin(polar), jnp.cos(polar)],
        axis=1,
    )


def look_up(table, index):
    onehot = (index[:, None] == jnp.arange(table.shape[0], dtype=jnp.int32)[None, :]).astype(
        jnp.float32
    )
    return jnp.dot(
        onehot, table, preferred_element_type=jnp.float32, precision=lax.Precision.HIGHEST
    )


def parent_turn(field, dirs, kappa):
    grid = jnp.asarray(node_table())
    angle = -kappa * (
        dirs[:, 0, None] * grid[0] + dirs[:, 1, None] * grid[1] + dirs[:, 2, None] * grid[2]
    )
    return rotate(field, jnp.cos(angle), jnp.sin(angle))


def split(values):
    high = lax.reduce_precision(values, 8, 7)
    return high.astype(jnp.bfloat16), (values - high).astype(jnp.bfloat16)


def level_partial(children, slots, parent_dirs, kappa, matrices):
    count = children.shape[0]
    owners = parent_dirs.shape[0]
    parents = jnp.transpose(slots).reshape(count)
    match = jnp.arange(owners, dtype=jnp.int32)[:, None] == parents[None, :]
    child_dirs = jnp.dot(
        jnp.transpose(match.astype(jnp.float32)),
        parent_dirs,
        preferred_element_type=jnp.float32,
        precision=lax.Precision.HIGHEST,
    )
    grid = jnp.asarray(octant_tables())
    grouped = child_dirs.reshape(count // 8, 8, 3)
    angle = (
        grouped[:, :, 0, None] * grid[None, :, 0]
        + grouped[:, :, 1, None] * grid[None, :, 1]
        + grouped[:, :, 2, None] * grid[None, :, 2]
    )
    angle = kappa * angle.reshape(count, 512)
    turned = rotate(children, jnp.cos(angle), jnp.sin(angle))
    moved = sum(
        jnp.einsum("jopn,omn->jopm", value, matrices, preferred_element_type=jnp.float32)
        for value in split(turned.reshape(count // 8, 8, 2, 512))
    )
    picks = match.astype(jnp.bfloat16)
    high, low = split(moved.reshape(count, 1024))
    total = jnp.dot(picks, high, preferred_element_type=jnp.float32) + jnp.dot(
        picks, low, preferred_element_type=jnp.float32
    )
    return total


def per_device(
    bin_points, bin_plan, bin_leaf, leaf_slots, box_slots, parent_cone, box_cone, cone_angles
):
    peers = lax.axis_size("sfc")
    groups = lax.axis_size("grp")
    group_rank = lax.axis_index("grp")
    leaf_count = leaf_slots.shape[2] * 8
    count = bin_points.shape[0]
    capacity = count // 8
    target = bin_plan[:, 0]
    number = jnp.arange(count, dtype=jnp.int32)
    ahead = (target[:, None] == target[None, :]) & (number[None, :] < number[:, None])
    position = target * capacity + jnp.sum(ahead.astype(jnp.int32), axis=1)
    taken = jnp.arange(peers * capacity, dtype=jnp.int32)[:, None] == position[None, :]
    order = jnp.sum(jnp.where(taken, number[None, :], 0), axis=1)
    labels = jnp.sum(jnp.where(taken, bin_leaf[None, :] + 1, 0), axis=1) - 1
    leaves = migrate(
        jnp.transpose(bin_points, (1, 0, 2)),
        order,
        labels.reshape(peers, capacity),
        "sfc",
        peers,
        leaf_count,
        0,
    ).reshape(leaf_count, 2, 512)
    matrices = jnp.asarray(child_matrices().astype(ml_dtypes.bfloat16))
    directions = cone_vectors(cone_angles)
    parent_dirs = look_up(directions, parent_cone[0])
    upper_dirs = look_up(directions, box_cone[0])
    first_owned = parent_dirs.shape[0] // groups
    second_owned = upper_dirs.shape[0] // groups
    partial_value = level_partial(leaves, leaf_slots[0], parent_dirs, kappa_leaf, matrices)
    summed = direct_scatter(partial_value, "grp", groups, 1).reshape(first_owned, 2, 512)
    mine = lax.dynamic_slice_in_dim(parent_dirs, group_rank * first_owned, first_owned, 0)
    first_level = parent_turn(summed, mine, kappa_leaf)
    slots_mine = lax.dynamic_slice_in_dim(
        box_slots[0], group_rank * (first_owned // 8), first_owned // 8, 1
    )
    upper = level_partial(first_level, slots_mine, upper_dirs, kappa_box, matrices)
    upper_owned = direct_scatter(upper, "grp", groups, 2).reshape(second_owned, 2, 512)
    upper_mine = lax.dynamic_slice_in_dim(upper_dirs, group_rank * second_owned, second_owned, 0)
    second_level = parent_turn(upper_owned, upper_mine, kappa_box)
    return (leaves, first_level, second_level)


def solution(mesh):
    placed = (
        P(("sfc", "grp"), None, None),
        P(("sfc", "grp"), None),
        P(("sfc", "grp")),
        P("sfc", None, "grp"),
        P("sfc", None, None),
        P("sfc", None),
        P("sfc", None),
        P(),
    )
    return jax.shard_map(
        per_device,
        mesh=mesh,
        in_specs=placed,
        out_specs=(
            P(("sfc", "grp"), None, None),
            P(("sfc", "grp"), None, None),
            P(("sfc", "grp"), None, None),
        ),
        check_vma=False,
    )
```
